32 devices in a mesh: groups: 2 (over x), chan: 16 (over z, y, core).
Axes of the slice: x: 2, y: 2, z: 4, core: 2. Of those that a mesh axis runs over, the one named last changes fastest.
Arguments:
- voltages: int32 [4096, 79, 2048], P(('groups', 'chan')), parts along dimension 0, may hold values from -96 to 96, as said below
- input_mask: int32 [4096], P(('groups', 'chan')), parts along dimension 0, may hold values 0 or 1
- fir_taps: float32 [16, 2048], replicated, may hold values from -1.5 to 1.5
Outputs:
- visibilities: bfloat16 [32768, 2048], P(('groups', 'chan')), parts along dimension 0
The draws below stay inside these ranges and needn't reach their ends.
There are 2 independent parts, one for each index of `groups`. The reference program is written for one: setup_inputs(seed, part) draws one part's arguments, and reference() takes and returns one part's arrays. A program takes and returns all parts, laid end to end along the dimension named above; an argument that names none is the same for every part. Nothing has to cross between parts.
Inputs may be any that keep to these rules, and one draw needn't show every extreme that they name: `voltages`: 8-bit voltage samples; each input's amplitude, colour and share of a common signal differ.
All inputs are finite; a program needn't handle non-finite values. No bound on the sum of `input_mask` on one device may be relied on, other than what follows from the above.
Results may differ from the reference program's by a relative error of at most 0.006.
Values may be sent and summed in bfloat16 or wider, within the bound.
A program may use at most 320 MiB of HBM per device.

```python
import math
import jax
import jax.numpy as jnp
from jax import lax

INPUTS = 2048
NFFT = 2048
TAPS = 16
SPEC = 64
CH = 8
FRAMES = 79


def draw_voltages(key, part):
    key_noise, key_colour, key_common, key_coupling = jax.random.split(key, 4)
    samples = FRAMES * NFFT
    input_index = jnp.arange(INPUTS, dtype=jnp.int32)[:, None]
    amplitude = 10 + 30 * input_index // max(INPUTS - 1, 1)
    uniform_bits = jax.random.randint(key_noise, (INPUTS, samples + 1), 0, 65536)
    own_noise = uniform_bits % (2 * amplitude + 1) - amplitude
    colour = jax.random.randint(key_colour, (INPUTS, 1), -1, 2)
    common = jax.random.randint(key_common, (1, samples), -16, 17)
    coupling = jax.random.randint(key_coupling, (INPUTS, 1), -1, 2)
    combined = own_noise[:, 1:] + colour * own_noise[:, :-1] + coupling * common
    combined = combined.at[INPUTS - 1, 0].set(96).at[0, 1].set(-96)
    return combined.reshape(INPUTS, FRAMES, NFFT).astype(jnp.int32)


def place_ends(array, key, smallest, high):
    spot = [jax.random.randint(jax.random.fold_in(key, axis), (), 0, length) for axis, length in enumerate(array.shape)]
    widest = array.shape.index(max(array.shape))
    next_to = spot[:widest] + [(spot[widest] + 1) % array.shape[widest]] + spot[widest + 1:]
    return array.at[tuple(spot)].set(smallest).at[tuple(next_to)].set(high)


def noise(key, dims, width, bound, held_as=jnp.bfloat16):
    array = width * jax.random.normal(key, dims, jnp.float32)
    return jnp.clip(array, min=-bound, max=bound).astype(held_as)


def setup_inputs(seed: int = 0, part: int = 0) -> dict:
    keys = jax.random.split(jax.random.key(seed), 4)
    part_splits = jax.random.split(jax.random.fold_in(keys[3], part), 4)
    voltages = draw_voltages(jax.random.fold_in(jax.random.fold_in(keys[3], part), 71), part)
    input_mask = place_ends((jax.random.randint(part_splits[1], (INPUTS,), 0, 16) < 15).astype(jnp.int32), jax.random.fold_in(part_splits[1], 1), 0, 1)
    fir_taps = noise(keys[2], (TAPS, NFFT), TAPS ** -0.5, 1.5, jnp.float32)
    return {"voltages": voltages, "input_mask": input_mask, "fir_taps": fir_taps}


def dft_matrix(length, channels):
    column = jnp.arange(length, dtype=jnp.int32)[:, None]
    channel = jnp.arange(1, channels + 1, dtype=jnp.int32)[None, :]
    phases = column * channel % length
    angles = phases.astype(jnp.float32) * (2.0 * math.pi / length)
    return jnp.concatenate([jnp.cos(angles), -jnp.sin(angles)], axis=1).astype(jnp.bfloat16)

def reference(voltages, input_mask, fir_taps):
    samples = voltages.astype(jnp.float32) * input_mask.astype(jnp.float32)[:, None, None]
    filtered = jnp.zeros((INPUTS, SPEC, NFFT), jnp.float32)
    for offset in range(TAPS):
        filtered = filtered + fir_taps[offset][None, None, :] * samples[:, offset:offset + SPEC, :]
    filtered = filtered.astype(jnp.bfloat16)
    spectra = jnp.dot(filtered.reshape(INPUTS * SPEC, NFFT), dft_matrix(NFFT, CH), preferred_element_type=jnp.float32).reshape(INPUTS, SPEC, 2 * CH)
    squares = lax.optimization_barrier(jnp.sum(spectra * spectra, axis=(0, 1)))
    power = squares[:CH] + squares[CH:]
    channel_gain = lax.rsqrt(power / (INPUTS * SPEC) + 1e-05)
    equalized = (spectra * jnp.concatenate([channel_gain, channel_gain])[None, None, :]).astype(jnp.bfloat16)
    by_channel = equalized.transpose(2, 0, 1)
    real_parts = by_channel[:CH]
    imag_parts = by_channel[CH:]

    def correlate(pair):
        real_part, imag_part = pair
        joined = jnp.concatenate([real_part, imag_part], axis=1)
        rotated = jnp.concatenate([imag_part, -real_part], axis=1)
        real_vis = jnp.dot(joined, joined.T, preferred_element_type=jnp.float32)
        imag_vis = jnp.dot(rotated, joined.T, preferred_element_type=jnp.float32)
        row_index = jnp.arange(INPUTS, dtype=jnp.int32)[:, None]
        column_index = jnp.arange(INPUTS, dtype=jnp.int32)[None, :]
        packed = jnp.where(column_index <= row_index, real_vis, imag_vis)
        return (packed / SPEC).astype(jnp.bfloat16)
    result = lax.map(correlate, (real_parts, imag_parts))
    return result.reshape(CH * INPUTS, INPUTS)
```

```python
import functools
import math

import jax
import jax.numpy as jnp
import numpy as np
from jax import lax
from jax.experimental import pallas as pl
from jax.experimental.pallas import tpu as pltpu
from jax.sharding import PartitionSpec as P

epsilon = 1e-05
FRAMES_PER_STEP = 4
VMEM_LIMIT = 56 * 1024 * 1024


def dft_rows(length, channels):
    column = np.arange(length)[None, :]
    channel = np.arange(1, channels + 1)[:, None]
    angles = (column * channel % length) * (2.0 * math.pi / length)
    return np.concatenate([np.cos(angles), -np.sin(angles)], axis=0)


def spectra_kernel(steps, v_ref, fir_ref, dft_ref, mask_ref, out_ref, w_ref, acc_ref):
    step = pl.program_id(0)
    per_step, inputs, length = v_ref.shape
    taps = fir_ref.shape[0]
    columns = dft_ref.shape[0]
    channels = columns // 2
    spectra = out_ref.shape[1] // 2

    @pl.when(step == 0)
    def _():
        for t in range(taps):
            w_ref[t * columns : (t + 1) * columns, :] = (
                fir_ref[t : t + 1, :] * dft_ref[...]
            ).astype(jnp.bfloat16)
        acc_ref[...] = jnp.zeros_like(acc_ref)

    samples = v_ref[...].astype(jnp.float32).astype(jnp.bfloat16)
    products = lax.dot_general(
        w_ref[...],
        samples.reshape(per_step * inputs, length),
        (((1,), (1,)), ((), ())),
        preferred_element_type=jnp.float32,
    )
    for place in range(per_step + taps - 1):
        terms = [
            products[t * columns : (t + 1) * columns, f * inputs : (f + 1) * inputs]
            for f in range(per_step)
            for t in range(taps)
            if f + taps - 1 - t == place
        ]
        acc_ref[step * per_step + place] += functools.reduce(jnp.add, terms)

    @pl.when(step == steps - 1)
    def _():
        mask = mask_ref[...].astype(jnp.float32)
        for c in range(channels):
            for part in range(2):
                column = part * channels + c
                values = acc_ref[taps - 1 : taps - 1 + spectra, column, :] * mask
                values = values.astype(jnp.bfloat16)
                rows = slice(part * spectra, (part + 1) * spectra)
                out_ref[2 * c, rows, :] = values
                out_ref[2 * c + 1, rows, :] = values


def visibility_kernel(count, rec_ref, out_ref, z_ref, rot_ref, scale_ref):
    step = pl.program_id(0)
    sources, depth, inputs = rec_ref.shape
    spectra = depth // 2
    rows = out_ref.shape[0]
    total = z_ref.shape[1]

    @pl.when(step == 0)
    def _():
        power = jnp.zeros((depth, inputs), jnp.float32)
        for source in range(sources):
            block = rec_ref[source]
            columns = slice(source * inputs, (source + 1) * inputs)
            z_ref[:, columns] = block
            rot_ref[:spectra, columns] = -block[spectra:]
            rot_ref[spectra:, columns] = block[:spectra]
            wide = block.astype(jnp.float32)
            power = power + wide * wide
        power = jnp.sum(jnp.sum(power, axis=0, keepdims=True), axis=1, keepdims=True)
        scale = 1.0 / ((power / count + epsilon) * spectra)
        scale_ref[...] = jnp.broadcast_to(scale, scale_ref.shape)

    parity = lax.axis_index("chan") % 2
    first = pl.multiple_of(parity * (total // 2) + step * rows, rows)
    left = z_ref[:, pl.ds(first, rows)].T
    scale = scale_ref[0:1, 0:1]
    width = 512
    for start in range(0, total, width):
        columns = slice(start, start + width)
        real = jnp.dot(left, z_ref[:, columns], preferred_element_type=jnp.float32)
        imag = jnp.dot(left, rot_ref[:, columns], preferred_element_type=jnp.float32)
        row = lax.broadcasted_iota(jnp.int32, real.shape, 0) + first
        column = lax.broadcasted_iota(jnp.int32, real.shape, 1) + start
        packed = jnp.where(column <= row, real, imag)
        out_ref[:, columns] = (packed * scale).astype(jnp.bfloat16)


def on_device(voltages, input_mask, fir_taps):
    devices = lax.axis_size("chan")
    channels = devices // 2
    inputs, frames, length = voltages.shape
    taps = fir_taps.shape[0]
    spectra = frames - taps + 1
    total = inputs * devices
    steps = pl.cdiv(frames, FRAMES_PER_STEP)
    by_frame = voltages.transpose(1, 0, 2)
    dft = jnp.asarray(dft_rows(length, channels), jnp.bfloat16).astype(jnp.float32)
    outgoing = pl.pallas_call(
        functools.partial(spectra_kernel, steps),
        out_shape=jax.ShapeDtypeStruct((devices, 2 * spectra, inputs), jnp.bfloat16),
        grid=(steps,),
        in_specs=[
            pl.BlockSpec((FRAMES_PER_STEP, inputs, length), lambda i: (i, 0, 0)),
            pl.BlockSpec((taps, length), lambda i: (0, 0)),
            pl.BlockSpec((2 * channels, length), lambda i: (0, 0)),
            pl.BlockSpec((1, inputs), lambda i: (0, 0)),
        ],
        out_specs=pl.BlockSpec((devices, 2 * spectra, inputs), lambda i: (0, 0, 0)),
        scratch_shapes=[
            pltpu.VMEM((taps * 2 * channels, length), jnp.bfloat16),
            pltpu.VMEM((steps * FRAMES_PER_STEP + taps - 1, 2 * channels, inputs), jnp.float32),
        ],
        compiler_params=pltpu.CompilerParams(vmem_limit_bytes=VMEM_LIMIT),
    )(by_frame, fir_taps, dft, input_mask[None, :])
    received = lax.all_to_all(outgoing, "chan", split_axis=0, concat_axis=0, tiled=True)
    rows = 128
    return pl.pallas_call(
        functools.partial(visibility_kernel, float(total * spectra)),
        out_shape=jax.ShapeDtypeStruct((total // 2, total), jnp.bfloat16),
        grid=(total // 2 // rows,),
        in_specs=[pl.BlockSpec((devices, 2 * spectra, inputs), lambda i: (0, 0, 0))],
        out_specs=pl.BlockSpec((rows, total), lambda i: (i, 0)),
        scratch_shapes=[
            pltpu.VMEM((2 * spectra, total), jnp.bfloat16),
            pltpu.VMEM((2 * spectra, total), jnp.bfloat16),
            pltpu.VMEM((8, 128), jnp.float32),
        ],
        compiler_params=pltpu.CompilerParams(vmem_limit_bytes=VMEM_LIMIT),
    )(received)


def solution(mesh):
    return jax.shard_map(
        on_device,
        mesh=mesh,
        in_specs=(P(("groups", "chan"), None, None), P(("groups", "chan")), P()),
        out_specs=P(("groups", "chan"), None),
        check_vma=False,
    )
```

```python
import functools
import math

import jax
import jax.numpy as jnp
import numpy as np
from jax import lax
from jax.experimental import pallas as pl
from jax.experimental.pallas import tpu as pltpu
from jax.sharding import PartitionSpec as P

epsilon = 1e-05
FRAMES_PER_STEP = 8
VMEM_LIMIT = 56 * 1024 * 1024


def dft_rows(length, channels):
    column = np.arange(length)[None, :]
    channel = np.arange(1, channels + 1)[:, None]
    angles = (column * channel % length) * (2.0 * math.pi / length)
    return np.concatenate([np.cos(angles), -np.sin(angles)], axis=0)


def spectra_kernel(
    steps, v_ref, fir_ref, dft_ref, mask_ref, out_ref,
    w_ref, acc_ref, stage_ref, send_sem, recv_sem, local_sem,
):
    step = pl.program_id(0)
    per_step, inputs, length = v_ref.shape
    taps = fir_ref.shape[0]
    columns = dft_ref.shape[0]
    channels = columns // 2
    barrier = pltpu.get_barrier_semaphore()

    @pl.when(step == 0)
    def _():
        here = lax.axis_index("chan")
        count = lax.axis_size("chan")

        def greet(offset, carry):
            pl.semaphore_signal(
                barrier,
                inc=1,
                device_id={"chan": lax.rem(here + offset, count)},
                device_id_type=pl.DeviceIdType.MESH,
            )
            return carry

        lax.fori_loop(1, count, greet, 0)
        for t in range(taps):
            w_ref[t * columns : (t + 1) * columns, :] = (
                fir_ref[t : t + 1, :] * dft_ref[...]
            ).astype(jnp.bfloat16)
        acc_ref[...] = jnp.zeros_like(acc_ref)

    samples = v_ref[...].astype(jnp.float32).astype(jnp.bfloat16)
    products = lax.dot_general(
        w_ref[...],
        samples.reshape(per_step * inputs, length),
        (((1,), (1,)), ((), ())),
        preferred_element_type=jnp.float32,
    )
    for place in range(per_step + taps - 1):
        terms = [
            products[t * columns : (t + 1) * columns, f * inputs : (f + 1) * inputs]
            for f in range(per_step)
            for t in range(taps)
            if f + taps - 1 - t == place
        ]
        acc_ref[step * per_step + place] += functools.reduce(jnp.add, terms)

    devices, pieces, depth, _ = out_ref.shape
    me = lax.axis_index("chan")
    piece = step - (per_step + taps - 2) // per_step

    @pl.when(piece == 0)
    def _():
        pl.semaphore_wait(barrier, devices - 1)

    @pl.when(piece >= 0)
    def _():
        mask = mask_ref[...].astype(jnp.float32)
        for c in range(channels):
            parts = [
                acc_ref[pl.ds(taps - 1 + piece * per_step, per_step), column, :]
                for column in (c, channels + c)
            ]
            stage_ref[c, piece] = (jnp.concatenate(parts, axis=0) * mask).astype(jnp.bfloat16)

        def send(offset, carry):
            target = lax.rem(me + offset, devices)
            pltpu.make_async_remote_copy(
                src_ref=stage_ref.at[target // 2, piece],
                dst_ref=out_ref.at[me, piece],
                send_sem=send_sem,
                recv_sem=recv_sem,
                device_id={"chan": target},
                device_id_type=pl.DeviceIdType.MESH,
            ).start()
            return carry

        lax.fori_loop(1, devices, send, 0)
        pltpu.make_async_copy(stage_ref.at[me // 2, piece], out_ref.at[me, piece], local_sem).start()

    @pl.when(step == steps - 1)
    def _():
        own = out_ref.at[0]
        others = out_ref.at[pl.ds(0, devices - 1)]
        pltpu.make_async_copy(own, own, local_sem).wait()
        pltpu.make_async_copy(others, others, send_sem).wait()
        pltpu.make_async_copy(others, others, recv_sem).wait()


def visibility_kernel(count, rec_ref, out_ref, z_ref, rot_ref, scale_ref):
    step = pl.program_id(0)
    sources, pieces, piece_depth, inputs = rec_ref.shape
    depth = pieces * piece_depth
    half = piece_depth // 2
    spectra = depth // 2
    rows = out_ref.shape[0]
    total = z_ref.shape[1]

    @pl.when(step == 0)
    def _():
        power = jnp.zeros((depth, inputs), jnp.float32)
        for source in range(sources):
            block = rec_ref[source]
            wide = block.astype(jnp.float32)
            turned = jnp.concatenate([-wide[:, half:], wide[:, :half]], axis=1)
            wide = wide.reshape(depth, inputs)
            columns = slice(source * inputs, (source + 1) * inputs)
            z_ref[:, columns] = block.reshape(depth, inputs)
            rot_ref[:, columns] = turned.reshape(depth, inputs).astype(jnp.bfloat16)
            power = power + wide * wide
        power = jnp.sum(jnp.sum(power, axis=0, keepdims=True), axis=1, keepdims=True)
        scale = 1.0 / ((power / count + epsilon) * spectra)
        scale_ref[...] = jnp.broadcast_to(scale, scale_ref.shape)

    parity = lax.axis_index("chan") % 2
    first = pl.multiple_of(parity * (total // 2) + step * rows, rows)
    left = z_ref[:, pl.ds(first, rows)].T
    scale = scale_ref[0:1, 0:1]
    width = 512
    for start in range(0, total, width):
        columns = slice(start, start + width)
        real = jnp.dot(left, z_ref[:, columns], preferred_element_type=jnp.float32)
        imag = jnp.dot(left, rot_ref[:, columns], preferred_element_type=jnp.float32)
        row = lax.broadcasted_iota(jnp.int32, real.shape, 0) + first
        column = lax.broadcasted_iota(jnp.int32, real.shape, 1) + start
        packed = jnp.where(column <= row, real, imag)
        out_ref[:, columns] = (packed * scale).astype(jnp.bfloat16)


def on_device(voltages, input_mask, fir_taps):
    devices = lax.axis_size("chan")
    channels = devices // 2
    inputs, frames, length = voltages.shape
    taps = fir_taps.shape[0]
    spectra = frames - taps + 1
    total = inputs * devices
    steps = pl.cdiv(frames, FRAMES_PER_STEP)
    by_frame = voltages.transpose(1, 0, 2)
    dft = jnp.asarray(dft_rows(length, channels), jnp.bfloat16).astype(jnp.float32)
    pieces = spectra // FRAMES_PER_STEP
    depth = 2 * FRAMES_PER_STEP
    columns = 2 * channels
    received = pl.pallas_call(
        functools.partial(spectra_kernel, steps),
        out_shape=jax.ShapeDtypeStruct((devices, pieces, depth, inputs), jnp.bfloat16),
        grid=(steps,),
        in_specs=[
            pl.BlockSpec((FRAMES_PER_STEP, inputs, length), lambda i: (i, 0, 0)),
            pl.BlockSpec((taps, length), lambda i: (0, 0)),
            pl.BlockSpec((columns, length), lambda i: (0, 0)),
            pl.BlockSpec((1, inputs), lambda i: (0, 0)),
        ],
        out_specs=pl.BlockSpec(memory_space=pl.ANY),
        scratch_shapes=[
            pltpu.VMEM((taps * columns, length), jnp.bfloat16),
            pltpu.VMEM((steps * FRAMES_PER_STEP + taps - 1, columns, inputs), jnp.float32),
            pltpu.VMEM((channels, pieces, depth, inputs), jnp.bfloat16),
            pltpu.SemaphoreType.DMA,
            pltpu.SemaphoreType.DMA,
            pltpu.SemaphoreType.DMA,
        ],
        compiler_params=pltpu.CompilerParams(
            vmem_limit_bytes=VMEM_LIMIT, collective_id=0, has_side_effects=True
        ),
    )(by_frame, fir_taps, dft, input_mask[None, :])
    rows = 128
    return pl.pallas_call(
        functools.partial(visibility_kernel, float(total * spectra)),
        out_shape=jax.ShapeDtypeStruct((total // 2, total), jnp.bfloat16),
        grid=(total // 2 // rows,),
        in_specs=[pl.BlockSpec((devices, pieces, depth, inputs), lambda i: (0, 0, 0, 0))],
        out_specs=pl.BlockSpec((rows, total), lambda i: (i, 0)),
        scratch_shapes=[
            pltpu.VMEM((2 * spectra, total), jnp.bfloat16),
            pltpu.VMEM((2 * spectra, total), jnp.bfloat16),
            pltpu.VMEM((8, 128), jnp.float32),
        ],
        compiler_params=pltpu.CompilerParams(vmem_limit_bytes=VMEM_LIMIT),
    )(received)


def solution(mesh):
    return jax.shard_map(
        on_device,
        mesh=mesh,
        in_specs=(P(("groups", "chan"), None, None), P(("groups", "chan")), P()),
        out_specs=P(("groups", "chan"), None),
        check_vma=False,
    )
```

```python
import functools
import math

import jax
import jax.numpy as jnp
import numpy as np
from jax import lax
from jax.experimental import pallas as pl
from jax.experimental.pallas import tpu as pltpu
from jax.sharding import PartitionSpec as P

epsilon = 1e-05
FRAMES_PER_STEP = 8
ROWS = 512
WIDTH = 512
VMEM_LIMIT = 56 * 1024 * 1024


def dft_rows(length, channels):
    column = np.arange(length)[None, :]
    channel = np.arange(1, channels + 1)[:, None]
    angles = (column * channel % length) * (2.0 * math.pi / length)
    return np.concatenate([np.cos(angles), -np.sin(angles)], axis=0)


def spectra_kernel(
    steps, v_ref, fir_ref, dft_ref, mask_ref, out_ref,
    w_ref, acc_ref, stage_ref, send_sem, recv_sem, local_sem,
):
    step = pl.program_id(0)
    per_step, inputs, length = v_ref.shape
    taps = fir_ref.shape[0]
    columns = dft_ref.shape[0]
    channels = columns // 2
    barrier = pltpu.get_barrier_semaphore()

    @pl.when(step == 0)
    def _():
        here = lax.axis_index("chan")
        count = lax.axis_size("chan")

        def greet(offset, carry):
            pl.semaphore_signal(
                barrier,
                inc=1,
                device_id={"chan": lax.rem(here + offset, count)},
                device_id_type=pl.DeviceIdType.MESH,
            )
            return carry

        lax.fori_loop(1, count, greet, 0)
        for t in range(taps):
            w_ref[t * columns : (t + 1) * columns, :] = (
                fir_ref[t : t + 1, :] * dft_ref[...]
            ).astype(jnp.bfloat16)
        acc_ref[...] = jnp.zeros_like(acc_ref)

    samples = v_ref[...].astype(jnp.float32).astype(jnp.bfloat16)
    products = lax.dot_general(
        w_ref[...],
        samples.reshape(per_step * inputs, length),
        (((1,), (1,)), ((), ())),
        preferred_element_type=jnp.float32,
    )
    for place in range(per_step + taps - 1):
        terms = [
            products[t * columns : (t + 1) * columns, f * inputs : (f + 1) * inputs]
            for f in range(per_step)
            for t in range(taps)
            if f + taps - 1 - t == place
        ]
        acc_ref[step * per_step + place] += functools.reduce(jnp.add, terms)

    devices, pieces, depth, _ = out_ref.shape
    me = lax.axis_index("chan")
    piece = step - (per_step + taps - 2) // per_step

    @pl.when(piece == 0)
    def _():
        pl.semaphore_wait(barrier, devices - 1)

    @pl.when(piece >= 0)
    def _():
        mask = mask_ref[...].astype(jnp.float32)
        for c in range(channels):
            parts = [
                acc_ref[pl.ds(taps - 1 + piece * per_step, per_step), column, :]
                for column in (c, channels + c)
            ]
            stage_ref[c, piece] = (jnp.concatenate(parts, axis=0) * mask).astype(jnp.bfloat16)

        def send(offset, carry):
            target = lax.rem(me + offset, devices)
            pltpu.make_async_remote_copy(
                src_ref=stage_ref.at[target // 2, piece],
                dst_ref=out_ref.at[me, piece],
                send_sem=send_sem,
                recv_sem=recv_sem,
                device_id={"chan": target},
                device_id_type=pl.DeviceIdType.MESH,
            ).start()
            return carry

        lax.fori_loop(1, devices, send, 0)
        pltpu.make_async_copy(stage_ref.at[me // 2, piece], out_ref.at[me, piece], local_sem).start()

    @pl.when(step == steps - 1)
    def _():
        own = out_ref.at[0]
        others = out_ref.at[pl.ds(0, devices - 1)]
        pltpu.make_async_copy(own, own, local_sem).wait()
        pltpu.make_async_copy(others, others, send_sem).wait()
        pltpu.make_async_copy(others, others, recv_sem).wait()


def visibility_kernel(count, rec_ref, out_ref, z_ref, mix_ref, scale_ref):
    step = pl.program_id(0)
    sources, pieces, piece_depth, inputs = rec_ref.shape
    depth = pieces * piece_depth
    half = piece_depth // 2
    spectra = depth // 2
    rows = out_ref.shape[0]
    total = z_ref.shape[1]
    start_row = (lax.axis_index("chan") % 2) * (total // 2)

    @pl.when(step == 0)
    def _():
        power = jnp.zeros((depth, inputs), jnp.float32)
        for source in range(sources):
            block = rec_ref[source]
            wide = block.astype(jnp.float32)
            turned = jnp.concatenate([-wide[:, half:], wide[:, :half]], axis=1)
            mixed = jnp.where(source * inputs < start_row, wide, turned)
            wide = wide.reshape(depth, inputs)
            columns = slice(source * inputs, (source + 1) * inputs)
            z_ref[:, columns] = block.reshape(depth, inputs)
            mix_ref[:, columns] = mixed.reshape(depth, inputs).astype(jnp.bfloat16)
            power = power + wide * wide
        power = jnp.sum(jnp.sum(power, axis=0, keepdims=True), axis=1, keepdims=True)
        scale = 1.0 / ((power / count + epsilon) * spectra)
        scale_ref[...] = jnp.broadcast_to(scale, scale_ref.shape)

    diagonal = pl.ds(pl.multiple_of(start_row + step * rows, rows), rows)
    own = z_ref[:, diagonal]
    left = own.T
    scale = scale_ref[0:1, 0:1]
    for start in range(0, total, WIDTH):
        columns = slice(start, start + WIDTH)
        values = jnp.dot(left, mix_ref[:, columns], preferred_element_type=jnp.float32)
        out_ref[:, columns] = (values * scale).astype(jnp.bfloat16)
    real = jnp.dot(left, own, preferred_element_type=jnp.float32) * scale
    row = lax.broadcasted_iota(jnp.int32, real.shape, 0)
    column = lax.broadcasted_iota(jnp.int32, real.shape, 1)
    imag = out_ref[:, diagonal].astype(jnp.float32)
    out_ref[:, diagonal] = jnp.where(column <= row, real, imag).astype(jnp.bfloat16)
    mix_ref[:, diagonal] = own


def on_device(voltages, input_mask, fir_taps):
    devices = lax.axis_size("chan")
    channels = devices // 2
    inputs, frames, length = voltages.shape
    taps = fir_taps.shape[0]
    spectra = frames - taps + 1
    total = inputs * devices
    steps = pl.cdiv(frames, FRAMES_PER_STEP)
    by_frame = voltages.transpose(1, 0, 2)
    dft = jnp.asarray(dft_rows(length, channels), jnp.bfloat16).astype(jnp.float32)
    pieces = spectra // FRAMES_PER_STEP
    depth = 2 * FRAMES_PER_STEP
    columns = 2 * channels
    received = pl.pallas_call(
        functools.partial(spectra_kernel, steps),
        out_shape=jax.ShapeDtypeStruct((devices, pieces, depth, inputs), jnp.bfloat16),
        grid=(steps,),
        in_specs=[
            pl.BlockSpec((FRAMES_PER_STEP, inputs, length), lambda i: (i, 0, 0)),
            pl.BlockSpec((taps, length), lambda i: (0, 0)),
            pl.BlockSpec((columns, length), lambda i: (0, 0)),
            pl.BlockSpec((1, inputs), lambda i: (0, 0)),
        ],
        out_specs=pl.BlockSpec(memory_space=pl.ANY),
        scratch_shapes=[
            pltpu.VMEM((taps * columns, length), jnp.bfloat16),
            pltpu.VMEM((steps * FRAMES_PER_STEP + taps - 1, columns, inputs), jnp.float32),
            pltpu.VMEM((channels, pieces, depth, inputs), jnp.bfloat16),
            pltpu.SemaphoreType.DMA,
            pltpu.SemaphoreType.DMA,
            pltpu.SemaphoreType.DMA,
        ],
        compiler_params=pltpu.CompilerParams(
            vmem_limit_bytes=VMEM_LIMIT, collective_id=0, has_side_effects=True
        ),
    )(by_frame, fir_taps, dft, input_mask[None, :])
    return pl.pallas_call(
        functools.partial(visibility_kernel, float(total * spectra)),
        out_shape=jax.ShapeDtypeStruct((total // 2, total), jnp.bfloat16),
        grid=(total // 2 // ROWS,),
        in_specs=[pl.BlockSpec((devices, pieces, depth, inputs), lambda i: (0, 0, 0, 0))],
        out_specs=pl.BlockSpec((ROWS, total), lambda i: (i, 0)),
        scratch_shapes=[
            pltpu.VMEM((2 * spectra, total), jnp.bfloat16),
            pltpu.VMEM((2 * spectra, total), jnp.bfloat16),
            pltpu.VMEM((8, 128), jnp.float32),
        ],
        compiler_params=pltpu.CompilerParams(vmem_limit_bytes=VMEM_LIMIT),
    )(received)


def solution(mesh):
    return jax.shard_map(
        on_device,
        mesh=mesh,
        in_specs=(P(("groups", "chan"), None, None), P(("groups", "chan")), P()),
        out_specs=P(("groups", "chan"), None),
        check_vma=False,
    )
```

```python
import functools
import math

import jax
import jax.numpy as jnp
import numpy as np
from jax import lax
from jax.experimental import pallas as pl
from jax.experimental.pallas import tpu as pltpu
from jax.sharding import PartitionSpec as P

epsilon = 1e-05
FRAMES_PER_STEP = 8
ROWS = 512
WIDTH = 512
VMEM_LIMIT = 28 * 1024 * 1024


def dft_rows(length, channels):
    column = np.arange(length)[None, :]
    channel = np.arange(1, channels + 1)[:, None]
    angles = (column * channel % length) * (2.0 * math.pi / length)
    return np.concatenate([np.cos(angles), -np.sin(angles)], axis=0)


def spectra_kernel(
    steps, v_ref, fir_ref, dft_ref, mask_ref, out_ref,
    w_ref, acc_ref, stage_ref, send_sem, recv_sem, local_sem,
):
    step = pl.program_id(0)
    per_step, inputs, length = v_ref.shape
    taps = fir_ref.shape[0]
    columns = dft_ref.shape[0]
    channels = columns // 2
    barrier = pltpu.get_barrier_semaphore()

    @pl.when(step == 0)
    def _():
        here = lax.axis_index("chan")
        count = lax.axis_size("chan")

        def greet(offset, carry):
            pl.semaphore_signal(
                barrier,
                inc=1,
                device_id={"chan": lax.rem(here + offset, count)},
                device_id_type=pl.DeviceIdType.MESH,
            )
            return carry

        lax.fori_loop(1, count, greet, 0)
        for t in range(taps):
            w_ref[t * columns : (t + 1) * columns, :] = (
                fir_ref[t : t + 1, :] * dft_ref[...]
            ).astype(jnp.bfloat16)
        acc_ref[...] = jnp.zeros_like(acc_ref)

    samples = v_ref[...].astype(jnp.float32).astype(jnp.bfloat16)
    products = lax.dot_general(
        w_ref[...],
        samples.reshape(per_step * inputs, length),
        (((1,), (1,)), ((), ())),
        preferred_element_type=jnp.float32,
    )
    for place in range(per_step + taps - 1):
        terms = [
            products[t * columns : (t + 1) * columns, f * inputs : (f + 1) * inputs]
            for f in range(per_step)
            for t in range(taps)
            if f + taps - 1 - t == place
        ]
        acc_ref[step * per_step + place] += functools.reduce(jnp.add, terms)

    devices, pieces, depth, _ = out_ref.shape
    me = lax.axis_index("chan")
    piece = step - (per_step + taps - 2) // per_step

    @pl.when(piece == 0)
    def _():
        pl.semaphore_wait(barrier, devices - 1)

    @pl.when(piece >= 0)
    def _():
        mask = mask_ref[...].astype(jnp.float32)
        for c in range(channels):
            parts = [
                acc_ref[pl.ds(taps - 1 + piece * per_step, per_step), column, :]
                for column in (c, channels + c)
            ]
            stage_ref[c, piece] = (jnp.concatenate(parts, axis=0) * mask).astype(jnp.bfloat16)

        def send(offset, carry):
            target = lax.rem(me + offset, devices)
            pltpu.make_async_remote_copy(
                src_ref=stage_ref.at[target // 2, piece],
                dst_ref=out_ref.at[me, piece],
                send_sem=send_sem,
                recv_sem=recv_sem,
                device_id={"chan": target},
                device_id_type=pl.DeviceIdType.MESH,
            ).start()
            return carry

        lax.fori_loop(1, devices, send, 0)
        pltpu.make_async_copy(stage_ref.at[me // 2, piece], out_ref.at[me, piece], local_sem).start()

    @pl.when(step == steps - 1)
    def _():
        own = out_ref.at[0]
        others = out_ref.at[pl.ds(0, devices - 1)]
        pltpu.make_async_copy(own, own, local_sem).wait()
        pltpu.make_async_copy(others, others, send_sem).wait()
        pltpu.make_async_copy(others, others, recv_sem).wait()


def visibility_kernel(count, rec_ref, out_ref, z_ref, mix_ref, scale_ref):
    step = pl.program_id(0)
    sources, pieces, piece_depth, inputs = rec_ref.shape
    depth = pieces * piece_depth
    half = piece_depth // 2
    spectra = depth // 2
    rows = out_ref.shape[0]
    total = z_ref.shape[1]
    start_row = (lax.axis_index("chan") % 2) * (total // 2)

    @pl.when(step == 0)
    def _():
        power = jnp.zeros((depth, inputs), jnp.float32)
        for source in range(sources):
            block = rec_ref[source]
            wide = block.astype(jnp.float32)
            turned = jnp.concatenate([-wide[:, half:], wide[:, :half]], axis=1)
            mixed = jnp.where(source * inputs < start_row, wide, turned)
            wide = wide.reshape(depth, inputs)
            columns = slice(source * inputs, (source + 1) * inputs)
            z_ref[:, columns] = block.reshape(depth, inputs)
            mix_ref[:, columns] = mixed.reshape(depth, inputs).astype(jnp.bfloat16)
            power = power + wide * wide
        power = jnp.sum(jnp.sum(power, axis=0, keepdims=True), axis=1, keepdims=True)
        scale = 1.0 / ((power / count + epsilon) * spectra)
        scale_ref[...] = jnp.broadcast_to(scale, scale_ref.shape)

    diagonal = pl.ds(pl.multiple_of(start_row + step * rows, rows), rows)
    own = z_ref[:, diagonal]
    left = own.T
    scale = scale_ref[0:1, 0:1]
    for start in range(0, total, WIDTH):
        columns = slice(start, start + WIDTH)
        values = jnp.dot(left, mix_ref[:, columns], preferred_element_type=jnp.float32)
        out_ref[:, columns] = (values * scale).astype(jnp.bfloat16)
    real = jnp.dot(left, own, preferred_element_type=jnp.float32) * scale
    row = lax.broadcasted_iota(jnp.int32, real.shape, 0)
    column = lax.broadcasted_iota(jnp.int32, real.shape, 1)
    imag = out_ref[:, diagonal].astype(jnp.float32)
    out_ref[:, diagonal] = jnp.where(column <= row, real, imag).astype(jnp.bfloat16)
    mix_ref[:, diagonal] = own


def on_device(voltages, input_mask, fir_taps):
    devices = lax.axis_size("chan")
    channels = devices // 2
    inputs, frames, length = voltages.shape
    taps = fir_taps.shape[0]
    spectra = frames - taps + 1
    total = inputs * devices
    steps = pl.cdiv(frames, FRAMES_PER_STEP)
    by_frame = voltages.transpose(1, 0, 2)
    dft = jnp.asarray(dft_rows(length, channels), jnp.bfloat16).astype(jnp.float32)
    pieces = spectra // FRAMES_PER_STEP
    depth = 2 * FRAMES_PER_STEP
    columns = 2 * channels
    received = pl.pallas_call(
        functools.partial(spectra_kernel, steps),
        out_shape=jax.ShapeDtypeStruct((devices, pieces, depth, inputs), jnp.bfloat16),
        grid=(steps,),
        in_specs=[
            pl.BlockSpec((FRAMES_PER_STEP, inputs, length), lambda i: (i, 0, 0)),
            pl.BlockSpec((taps, length), lambda i: (0, 0)),
            pl.BlockSpec((columns, length), lambda i: (0, 0)),
            pl.BlockSpec((1, inputs), lambda i: (0, 0)),
        ],
        out_specs=pl.BlockSpec(memory_space=pl.ANY),
        scratch_shapes=[
            pltpu.VMEM((taps * columns, length), jnp.bfloat16),
            pltpu.VMEM((steps * FRAMES_PER_STEP + taps - 1, columns, inputs), jnp.float32),
            pltpu.VMEM((channels, pieces, depth, inputs), jnp.bfloat16),
            pltpu.SemaphoreType.DMA,
            pltpu.SemaphoreType.DMA,
            pltpu.SemaphoreType.DMA,
        ],
        compiler_params=pltpu.CompilerParams(
            vmem_limit_bytes=VMEM_LIMIT, collective_id=0, has_side_effects=True
        ),
    )(by_frame, fir_taps, dft, input_mask[None, :])
    return pl.pallas_call(
        functools.partial(visibility_kernel, float(total * spectra)),
        out_shape=jax.ShapeDtypeStruct((total // 2, total), jnp.bfloat16),
        grid=(total // 2 // ROWS,),
        in_specs=[pl.BlockSpec((devices, pieces, depth, inputs), lambda i: (0, 0, 0, 0))],
        out_specs=pl.BlockSpec((ROWS, total), lambda i: (i, 0)),
        scratch_shapes=[
            pltpu.VMEM((2 * spectra, total), jnp.bfloat16),
            pltpu.VMEM((2 * spectra, total), jnp.bfloat16),
            pltpu.VMEM((8, 128), jnp.float32),
        ],
        compiler_params=pltpu.CompilerParams(vmem_limit_bytes=VMEM_LIMIT),
    )(received)


def solution(mesh):
    return jax.shard_map(
        on_device,
        mesh=mesh,
        in_specs=(P(("groups", "chan"), None, None), P(("groups", "chan")), P()),
        out_specs=P(("groups", "chan"), None),
        check_vma=False,
    )
```
